512 devices in a mesh: band: 32 (over x, y_hi, core), tm: 16 (over y_lo, z).
Axes of the slice: x: 4, y: 8 (y_hi: 4, y_lo: 2; y = y_hi * 2 + y_lo), z: 8, core: 2. Of those that a mesh axis runs over, the one named last changes fastest.
Arguments:
- partial_sums: float32 [4096, 16384], P('band', 'tm'), may hold values from -6 to 6
- delays: int32 [5, 4096], replicated, may hold values from 0 to 96, as said below
Outputs:
- best_snr: float32 [4096, 16384], P(None, ('tm', 'band'))
The draws below stay inside these ranges and needn't reach their ends.
Inputs may be any that keep to these rules, and one draw needn't show every extreme that they name: Whole delays from the channel frequencies and a range of trial dispersion measures, never falling with the merged row within each subband; the top row of the last section has exactly 96.
All inputs are finite; a program needn't handle non-finite values.
Results may differ from the reference program's by a relative error of at most 0.00002.
Values sent between devices are 32-bit elements; how exact they have to be, the bound alone decides.
No kernel may reach another device: no remote copies, remote signals or barrier semaphores. Data moves between devices by JAX's collectives and lax.ppermute only.
A program may use at most 128 MiB of HBM per device.

```python
import math
import jax
import jax.numpy as jnp
from jax import lax

NCHAN = 4096
R = 128
HALO = 96
WMAX = 64
SECTIONS = 5
NDM = 4096
TIME = 16384
N_BAND = 32


def draw_delays(key, part):
    key = jax.random.fold_in(key, 11)
    base_key, step_key, offset_key = jax.random.split(key, 3)
    lowest = jax.random.randint(base_key, (), 1024, 8192, dtype=jnp.int32)
    spacing = jax.random.randint(step_key, (), 1, 9, dtype=jnp.int32)
    dm_low = jax.random.randint(offset_key, (), 0, NDM, dtype=jnp.int32)
    band_count = NDM // R
    chans_dev = NCHAN // band_count

    def inverse_square(channel):
        frequency = lowest + channel * spacing
        return jnp.int32(1073741824) // (frequency * frequency // 1024)
    overall = inverse_square(jnp.int32(0)) - inverse_square(jnp.int32(NCHAN // 2))
    row_ids = jnp.arange(NDM, dtype=jnp.int32)
    tables = []
    for section_idx in range(SECTIONS):
        group_size = 2 ** (section_idx + 1)
        span_rows = R * group_size
        merged_idx = row_ids // span_rows
        dm_row = row_ids % span_rows
        start_chan = merged_idx * (chans_dev * group_size)
        mid_chan = start_chan + chans_dev * group_size // 2
        delay_gap = inverse_square(start_chan) - inverse_square(mid_chan)
        scaled = HALO * delay_gap // overall
        trial = dm_row * (band_count // group_size)
        tables.append((dm_low + trial) * scaled // (dm_low + NDM - 1))
    return jnp.stack(tables).astype(jnp.int32)


def steps_of(own_key, extent, shards, smallest, top_value):
    level, own = 1.0, jax.random.fold_in(own_key, 6)
    for position, blocks in shards:
        heights = jnp.exp(jax.random.uniform(jax.random.fold_in(own, position), (blocks,), jnp.float32, smallest / len(shards), top_value / len(shards)))
        level = level * jnp.repeat(heights, extent[position] // blocks).reshape([-1 if axis == position else 1 for axis in range(len(extent))])
    return level


def noise(own_key, extent, spread, reach, cuts=(), kind=jnp.bfloat16):
    array = spread * jax.random.normal(own_key, extent, jnp.float32)
    if cuts:
        array = array * steps_of(own_key, extent, cuts, -0.22, 0.18)
    return jnp.clip(array, -reach, reach).astype(kind)


def setup_inputs(seed: int = 0) -> dict:
    splits = jax.random.split(jax.random.key(seed), 3)
    return {
        "partial_sums": noise(splits[0], (NDM, TIME), 1.0, 6.0, ((0, 32), (1, 16)), jnp.float32),
        "delays": draw_delays(jax.random.fold_in(splits[2], 71), 0),
    }


def shifted_rows(row_data, delay_rows, rim_span):
    row_count = row_data.shape[0]
    time_width = row_data.shape[1]
    block_rows = math.gcd(row_count, 256)
    padded = jnp.pad(row_data, ((0, 0), (0, rim_span)))
    padded = padded.reshape(row_count // block_rows, block_rows, time_width + rim_span)
    offsets = delay_rows.reshape(row_count // block_rows, block_rows)

    def one_block(pair_item):
        row_piece, row_shift = pair_item
        col_index = jnp.arange(time_width, dtype=jnp.int32)[None, :] + row_shift[:, None]
        return jnp.take_along_axis(row_piece, col_index, axis=1)
    return lax.map(one_block, (padded, offsets)).reshape(row_count, time_width)

def reference(partial_sums, delays):
    fields = partial_sums
    time_len = fields.shape[1]
    for section_idx in range(SECTIONS):
        group_size = 2 ** (section_idx + 1)
        merged = NDM // (R * group_size)
        halves = fields.reshape(merged, 2, R * group_size // 2, time_len)
        lower_rep = jnp.repeat(halves[:, 0], 2, axis=1).reshape(NDM, time_len)
        upper_rep = jnp.repeat(halves[:, 1], 2, axis=1).reshape(NDM, time_len)
        fields = upper_rep + shifted_rows(lower_rep, delays[section_idx], HALO)
    box_sums = jnp.pad(fields, ((0, 0), (WMAX, 0)))
    best_snr = box_sums[:, WMAX:] * (1.0 / math.sqrt(N_BAND))
    box_width = 1
    while box_width < WMAX:
        box_sums = box_sums[:, box_width:] + box_sums[:, :-box_width]
        box_width = box_width * 2
        best_snr = jnp.maximum(best_snr, box_sums[:, box_sums.shape[1] - time_len:] * (1.0 / math.sqrt(box_width * N_BAND)))
    return best_snr
```

```python
import functools
import math

import jax
import jax.numpy as jnp
from jax import lax
from jax.experimental import pallas as pl
from jax.experimental.pallas import tpu as pltpu
from jax.sharding import PartitionSpec as P

HALO = 96
WMAX = 64
LANES = 128
SLOTS = 16


def shifted(value, axis, steps):
    count = lax.axis_size(axis)
    initial, last = (max(0, -steps), min(count, count - steps))
    return lax.ppermute(value, axis, [(source, source + steps) for source in range(initial, last)])


def pack_kernel(sections, band_count, x_ref, delays_ref, out_ref, shifts_ref):
    rows, cols = x_ref.shape
    blocks = cols // LANES
    part = rows // band_count
    for chunk in range(band_count):
        for block in range(blocks):
            start = chunk * part * blocks + block * part
            out_ref[start : start + part, :] = x_ref[
                chunk * part : chunk * part + part, block * LANES : (block + 1) * LANES
            ]
    my_band = lax.axis_index("band")
    lane = lax.broadcasted_iota(jnp.int32, (1, LANES), 1)
    for section_idx in range(sections):
        group = 2 << section_idx
        span = part * group
        first = my_band * span
        line = jnp.zeros((1, LANES), jnp.int32)
        for merged in range(band_count // group):
            column = pl.multiple_of(merged * group * LANES + first // LANES * LANES, LANES)
            values = delays_ref[section_idx : section_idx + 1, pl.ds(column, LANES)]
            turn = lax.rem(merged * span - lax.rem(first, LANES) + LANES, LANES)
            values = pltpu.roll(values, turn, 1)
            line = jnp.where((lane >= merged * span) & (lane < (merged + 1) * span), values, line)
        shifts_ref[section_idx : section_idx + 1, :] = line


def pack(x, delays, sections, band_count):
    rows, cols = x.shape
    return pl.pallas_call(
        functools.partial(pack_kernel, sections, band_count),
        out_shape=[
            jax.ShapeDtypeStruct((rows * cols // LANES, LANES), x.dtype),
            jax.ShapeDtypeStruct((sections, LANES), jnp.int32),
        ],
        in_specs=[pl.BlockSpec(memory_space=pltpu.VMEM)] * 2,
        out_specs=[pl.BlockSpec(memory_space=pltpu.VMEM)] * 2,
        compiler_params=pltpu.CompilerParams(vmem_limit_bytes=16 * 2**20),
    )(x, delays)


def merge_kernel(sections, band_count, delays_ref, main_ref, right_ref, left_ref, out_ref, ping, pong, turned):
    rows = LANES
    part = rows // band_count
    blocks = main_ref.shape[0] // rows
    right_blocks = right_ref.shape[0] // rows
    left_blocks = left_ref.shape[0] // rows
    time_len = blocks * LANES
    lane = lax.broadcasted_iota(jnp.int32, (8, LANES), 1)
    slot = lax.broadcasted_iota(jnp.int32, (8, LANES), 0)
    last_slot = slot == 7

    def fill(row, _):
        chunk, local = row // part, lax.rem(row, part)
        ping[row, 0:blocks, :] = main_ref[pl.ds(chunk * blocks * part + local, blocks, stride=part), :]
        ping[row, blocks : blocks + right_blocks, :] = right_ref[
            pl.ds(chunk * right_blocks * part + local, right_blocks, stride=part), :
        ]
        ping[row, SLOTS - 1 : SLOTS, :] = left_ref[pl.ds((chunk * left_blocks + left_blocks - 1) * part + local, 1), :]
        return 0

    lax.fori_loop(0, rows, fill, 0, unroll=8)

    source, target = ping, pong
    for section_idx in range(sections):
        span = (rows // band_count) << (section_idx + 1)
        half = span // 2

        def merge(step, _, source=source, target=target, half=half, span=span, section_idx=section_idx):
            within = lax.rem(step, half)
            base = step * 2 - within * 2
            lower = base + within
            upper = lower + half
            low_a = source[lower, 0:8, :]
            low_b = source[lower, 8:16, :]
            up_a = source[upper, 0:8, :]
            up_b = source[upper, 8:16, :]
            roll_a = pltpu.roll(low_a, 7, 0)
            roll_b = pltpu.roll(low_b, 7, 0)
            next_a = jnp.where(last_slot, roll_b, roll_a)
            next_b = jnp.where(last_slot, roll_a, roll_b)
            for side in range(2):
                row = base + within * 2 + side
                delay = delays_ref[section_idx, row]
                turn = lax.rem(LANES - delay, LANES)
                own = lane >= delay
                target[row, 0:8, :] = up_a + pltpu.roll(jnp.where(own, low_a, next_a), turn, 1)
                target[row, 8:16, :] = up_b + pltpu.roll(jnp.where(own, low_b, next_b), turn, 1)
            return 0

        lax.fori_loop(0, rows // 2, merge, 0, unroll=8)
        source, target = target, source

    flat = source.reshape(rows * SLOTS, LANES)
    before = flat[pl.ds(SLOTS - 1, rows, stride=SLOTS), :].T
    keep = lax.axis_index("tm") > 0
    turned[0:WMAX, :] = jnp.where(keep, before[LANES - WMAX :, :], 0.0)
    for block in range(blocks):
        turned[WMAX + block * LANES : WMAX + (block + 1) * LANES, :] = flat[
            pl.ds(block, rows, stride=SLOTS), :
        ].T

    piece = 64

    def detect(index, _):
        start = pl.multiple_of(index * piece, piece)
        sums = turned[pl.ds(start, piece + WMAX), :]
        best = sums[WMAX:, :] * (1.0 / math.sqrt(band_count))
        width = 1
        while width < WMAX:
            sums = sums + pltpu.roll(sums, width, 0)
            width *= 2
            best = jnp.maximum(best, sums[WMAX:, :] * (1.0 / math.sqrt(width * band_count)))
        out_ref[pl.ds(start, piece), :] = best
        return 0

    lax.fori_loop(0, time_len // piece, detect, 0)


def body(partial_sums, delays):
    band_count = lax.axis_size("band")
    sections = band_count.bit_length() - 1
    rows, cols = partial_sums.shape
    blocks = cols // LANES
    part = rows // band_count
    packed, shifts = pack(partial_sums, delays, sections, band_count)
    mine = lax.all_to_all(packed.reshape(band_count, part * blocks, LANES), "band", split_axis=0, concat_axis=0, tiled=True)
    right_blocks = -(-HALO * sections // LANES)
    right = shifted(mine[:, : right_blocks * part], "tm", -1)
    left = shifted(mine[:, (blocks - 2) * part :], "tm", 1)

    best = pl.pallas_call(
        functools.partial(merge_kernel, sections, band_count),
        out_shape=jax.ShapeDtypeStruct((cols, rows), jnp.float32),
        in_specs=[pl.BlockSpec(memory_space=pltpu.SMEM)] + [pl.BlockSpec(memory_space=pltpu.VMEM)] * 3,
        out_specs=pl.BlockSpec(memory_space=pltpu.VMEM),
        scratch_shapes=[
            pltpu.VMEM((rows, SLOTS, LANES), jnp.float32),
            pltpu.VMEM((rows, SLOTS, LANES), jnp.float32),
            pltpu.VMEM((WMAX + cols, rows), jnp.float32),
        ],
        compiler_params=pltpu.CompilerParams(vmem_limit_bytes=32 * 2**20),
    )(shifts, *(piece.reshape(-1, LANES) for piece in (mine, right, left)))

    slabs = best.reshape(band_count, cols // band_count, rows)
    slabs = lax.all_to_all(slabs, "band", split_axis=0, concat_axis=0, tiled=True)
    return slabs.transpose(1, 0, 2).reshape(cols // band_count, band_count * rows).T


def solution(mesh):
    in_specs = (P("band", "tm"), P())
    out_specs = P(None, ("tm", "band"))
    return jax.shard_map(body, mesh=mesh, in_specs=in_specs, out_specs=out_specs, check_vma=False)
```

```python
import functools
import math

import jax
import jax.numpy as jnp
from jax import lax
from jax.experimental import pallas as pl
from jax.experimental.pallas import tpu as pltpu
from jax.sharding import PartitionSpec as P

HALO = 96
WMAX = 64
LANES = 128
SLOTS = 16
VMEM = pl.BlockSpec(memory_space=pltpu.VMEM)
SMEM = pl.BlockSpec(memory_space=pltpu.SMEM)


def shifted(value, axis, steps):
    count = lax.axis_size(axis)
    initial, last = (max(0, -steps), min(count, count - steps))
    return lax.ppermute(value, axis, [(source, source + steps) for source in range(initial, last)])


def right_blocks(band_count):
    sections = band_count.bit_length() - 1
    return [-(-HALO * (sections - bin(band).count("1")) // LANES) for band in range(band_count)]


def pack_kernel(x_ref, out_ref):
    rows, cols = x_ref.shape
    blocks = cols // LANES
    for group in range(rows // 8):
        for block in range(blocks):
            out_ref[pl.ds(group * 8 * blocks + block, 8, stride=blocks), :] = x_ref[
                group * 8 : group * 8 + 8, block * LANES : (block + 1) * LANES
            ]


def delays_kernel(sections, band_count, part, delays_ref, shifts_ref):
    my_band = lax.axis_index("band")
    lane = lax.broadcasted_iota(jnp.int32, (1, LANES), 1)
    for section_idx in range(sections):
        group = 2 << section_idx
        span = part * group
        first = my_band * span
        line = jnp.zeros((1, LANES), jnp.int32)
        for merged in range(band_count // group):
            column = pl.multiple_of(merged * group * LANES + first // LANES * LANES, LANES)
            values = delays_ref[section_idx : section_idx + 1, pl.ds(column, LANES)]
            turn = lax.rem(merged * span - lax.rem(first, LANES) + LANES, LANES)
            values = pltpu.roll(values, turn, 1)
            line = jnp.where((lane >= merged * span) & (lane < (merged + 1) * span), values, line)
        shifts_ref[section_idx : section_idx + 1, :] = line


def rims_kernel(counts, part, blocks, main_ref, right_ref, left_ref):
    place = 0
    for row in range(len(counts) * part):
        count = counts[row // part]
        if count:
            right_ref[place : place + count, :] = main_ref[row * blocks : row * blocks + count, :]
        place += count
        left_ref[row : row + 1, :] = main_ref[row * blocks + blocks - 1 : row * blocks + blocks, :]


def merge_kernel(sections, counts, part, blocks, shifts_ref, main_ref, right_ref, left_ref, out_ref, *scratch):
    ping_a, ping_b, pong_a, pong_b, turned = scratch
    band_count = len(counts)
    rows = band_count * part
    time_len = blocks * LANES
    lane = lax.broadcasted_iota(jnp.int32, (8, LANES), 1)
    last_slot = lax.broadcasted_iota(jnp.int32, (8, LANES), 0) == 7

    place = 0
    for row in range(rows):
        count = counts[row // part]
        if count:
            ping_b[row * 8 : row * 8 + count, :] = right_ref[place : place + count, :]
        place += count
        ping_b[row * 8 + 7 : row * 8 + 8, :] = left_ref[row : row + 1, :]

    source, target = (main_ref, ping_b), (pong_a, pong_b)
    for section_idx in range(sections):
        half = part << section_idx
        for step in range(rows // 2):
            within = step % half
            base = (step - within) * 2
            lower = (base + within) * 8
            upper = lower + half * 8
            low_a = source[0][lower : lower + 8, :]
            low_b = source[1][lower : lower + 8, :]
            roll_a = pltpu.roll(low_a, 7, 0)
            roll_b = pltpu.roll(low_b, 7, 0)
            next_a = jnp.where(last_slot, roll_b, roll_a)
            next_b = jnp.where(last_slot, roll_a, roll_b)
            up_a = source[0][upper : upper + 8, :]
            up_b = source[1][upper : upper + 8, :]
            for side in range(2):
                row = base + within * 2 + side
                delay = shifts_ref[section_idx, row]
                turn = (LANES - delay) & (LANES - 1)
                own = lane >= delay
                target[0][row * 8 : row * 8 + 8, :] = up_a + pltpu.roll(jnp.where(own, low_a, next_a), turn, 1)
                target[1][row * 8 : row * 8 + 8, :] = up_b + pltpu.roll(jnp.where(own, low_b, next_b), turn, 1)
        source, target = target, ((ping_a, ping_b) if section_idx % 2 == 0 else (pong_a, pong_b))

    before = source[1][pl.ds(7, rows, stride=8), :].T
    turned[0:WMAX, :] = jnp.where(lax.axis_index("tm") > 0, before[LANES - WMAX :, :], 0.0)
    for block in range(blocks):
        turned[WMAX + block * LANES : WMAX + (block + 1) * LANES, :] = source[0][pl.ds(block, rows, stride=8), :].T

    for start in range(0, time_len, LANES):
        sums = turned[start : start + LANES + WMAX, :]
        best = sums[WMAX:, :] * (1.0 / math.sqrt(band_count))
        width = 1
        while width < WMAX:
            sums = sums + pltpu.roll(sums, width, 0)
            width *= 2
            best = jnp.maximum(best, sums[WMAX:, :] * (1.0 / math.sqrt(width * band_count)))
        out_ref[start : start + LANES, :] = best


def body(partial_sums, delays):
    band_count = lax.axis_size("band")
    sections = band_count.bit_length() - 1
    rows, cols = partial_sums.shape
    blocks = cols // LANES
    part = rows // band_count
    counts = right_blocks(band_count)
    params = pltpu.CompilerParams(vmem_limit_bytes=24 * 2**20)

    def struct(*shape, dtype=jnp.float32):
        return jax.ShapeDtypeStruct(shape, dtype)

    packed = pl.pallas_call(
        pack_kernel,
        out_shape=struct(rows * blocks, LANES),
        in_specs=[VMEM],
        out_specs=VMEM,
        compiler_params=params,
    )(partial_sums)
    shifts = pl.pallas_call(
        functools.partial(delays_kernel, sections, band_count, part),
        out_shape=struct(sections, LANES, dtype=jnp.int32),
        in_specs=[VMEM],
        out_specs=VMEM,
        compiler_params=params,
    )(delays)

    mine = lax.all_to_all(packed.reshape(band_count, part * blocks, LANES), "band", split_axis=0, concat_axis=0, tiled=True)
    mine = mine.reshape(rows * blocks, LANES)
    right, left = pl.pallas_call(
        functools.partial(rims_kernel, counts, part, blocks),
        out_shape=[struct(sum(counts) * part, LANES), struct(rows, LANES)],
        in_specs=[VMEM],
        out_specs=[VMEM] * 2,
        compiler_params=params,
    )(mine)
    right = shifted(right, "tm", -1)
    left = shifted(left, "tm", 1)

    best = pl.pallas_call(
        functools.partial(merge_kernel, sections, counts, part, blocks),
        out_shape=struct(cols, rows),
        in_specs=[SMEM] + [VMEM] * 3,
        out_specs=VMEM,
        scratch_shapes=[pltpu.VMEM((rows * 8, LANES), jnp.float32)] * 4 + [pltpu.VMEM((WMAX + cols, rows), jnp.float32)],
        compiler_params=params,
    )(shifts, mine, right, left)

    slabs = best.reshape(band_count, cols // band_count, rows)
    slabs = lax.all_to_all(slabs, "band", split_axis=0, concat_axis=0, tiled=True)
    return slabs.transpose(1, 0, 2).reshape(cols // band_count, band_count * rows).T


def solution(mesh):
    in_specs = (P("band", "tm"), P())
    out_specs = P(None, ("tm", "band"))
    return jax.shard_map(body, mesh=mesh, in_specs=in_specs, out_specs=out_specs, check_vma=False)
```

```python
import functools
import math

import jax
import jax.numpy as jnp
from jax import lax
from jax.experimental import pallas as pl
from jax.experimental.pallas import tpu as pltpu
from jax.sharding import PartitionSpec as P

HALO = 96
WMAX = 64
LANES = 128
SLOTS = 16
VMEM = pl.BlockSpec(memory_space=pltpu.VMEM)
SMEM = pl.BlockSpec(memory_space=pltpu.SMEM)


def right_blocks(band_count):
    sections = band_count.bit_length() - 1
    return [-(-HALO * (sections - bin(band).count("1")) // LANES) for band in range(band_count)]


def pack_kernel(x_ref, out_ref):
    rows, cols = x_ref.shape
    blocks = cols // LANES
    for group in range(rows // 8):
        for block in range(blocks):
            out_ref[pl.ds(group * 8 * blocks + block, 8, stride=blocks), :] = x_ref[
                group * 8 : group * 8 + 8, block * LANES : (block + 1) * LANES
            ]


def delays_kernel(sections, band_count, part, delays_ref, shifts_ref):
    my_band = lax.axis_index("band")
    lane = lax.broadcasted_iota(jnp.int32, (1, LANES), 1)
    for section_idx in range(sections):
        group = 2 << section_idx
        span = part * group
        first = my_band * span
        line = jnp.zeros((1, LANES), jnp.int32)
        for merged in range(band_count // group):
            column = pl.multiple_of(merged * group * LANES + first // LANES * LANES, LANES)
            values = delays_ref[section_idx : section_idx + 1, pl.ds(column, LANES)]
            turn = lax.rem(merged * span - lax.rem(first, LANES) + LANES, LANES)
            values = pltpu.roll(values, turn, 1)
            line = jnp.where((lane >= merged * span) & (lane < (merged + 1) * span), values, line)
        shifts_ref[section_idx : section_idx + 1, :] = line


def rims_kernel(counts, part, blocks, main_ref, right_ref, left_ref, middle_ref):
    place = 0
    for row in range(len(counts) * part):
        count = counts[row // part]
        if count:
            right_ref[place : place + count, :] = main_ref[row * blocks : row * blocks + count, :]
        place += count
        last = main_ref[row * blocks + blocks - 1 : row * blocks + blocks, :]
        left_ref[row : row + 1, :] = last
        middle_ref[row : row + 1, :] = last


def merge_kernel(sections, counts, part, blocks, shifts_ref, main_ref, right_ref, left_ref, middle_ref, out_ref, *scratch):
    ping_a, ping_b, pong_a, pong_b, turned = scratch
    band_count = len(counts)
    rows = band_count * part
    time_len = blocks * LANES
    lane = lax.broadcasted_iota(jnp.int32, (8, LANES), 1)
    last_slot = lax.broadcasted_iota(jnp.int32, (8, LANES), 0) == 7

    place = 0
    for row in range(rows):
        count = counts[row // part]
        if count:
            ping_b[row * 8 : row * 8 + count, :] = right_ref[place : place + count, :]
        place += count

    def gather(ref):
        for row in range(rows):
            ping_b[row * 8 + 7 : row * 8 + 8, :] = ref[row : row + 1, :]

    beyond = lax.axis_index("tm") - lax.axis_size("tm") // 2
    on_middle = (beyond == 0) | (beyond == 1)
    pl.when(on_middle)(lambda: gather(middle_ref))
    pl.when(jnp.logical_not(on_middle))(lambda: gather(left_ref))

    source, target = (main_ref, ping_b), (pong_a, pong_b)
    for section_idx in range(sections):
        half = part << section_idx
        for step in range(rows // 2):
            within = step % half
            base = (step - within) * 2
            lower = (base + within) * 8
            upper = lower + half * 8
            low_a = source[0][lower : lower + 8, :]
            low_b = source[1][lower : lower + 8, :]
            roll_a = pltpu.roll(low_a, 7, 0)
            roll_b = pltpu.roll(low_b, 7, 0)
            next_a = jnp.where(last_slot, roll_b, roll_a)
            next_b = jnp.where(last_slot, roll_a, roll_b)
            up_a = source[0][upper : upper + 8, :]
            up_b = source[1][upper : upper + 8, :]
            for side in range(2):
                row = base + within * 2 + side
                delay = shifts_ref[section_idx, row]
                turn = (LANES - delay) & (LANES - 1)
                own = lane >= delay
                target[0][row * 8 : row * 8 + 8, :] = up_a + pltpu.roll(jnp.where(own, low_a, next_a), turn, 1)
                target[1][row * 8 : row * 8 + 8, :] = up_b + pltpu.roll(jnp.where(own, low_b, next_b), turn, 1)
        source, target = target, ((ping_a, ping_b) if section_idx % 2 == 0 else (pong_a, pong_b))

    before = source[1][pl.ds(7, rows, stride=8), :].T
    turned[0:WMAX, :] = jnp.where(lax.axis_index("tm") > 0, before[LANES - WMAX :, :], 0.0)
    for block in range(blocks):
        turned[WMAX + block * LANES : WMAX + (block + 1) * LANES, :] = source[0][pl.ds(block, rows, stride=8), :].T

    for start in range(0, time_len, LANES):
        sums = turned[start : start + LANES + WMAX, :]
        best = sums[WMAX:, :] * (1.0 / math.sqrt(band_count))
        width = 1
        while width < WMAX:
            sums = sums + pltpu.roll(sums, width, 0)
            width *= 2
            best = jnp.maximum(best, sums[WMAX:, :] * (1.0 / math.sqrt(width * band_count)))
        out_ref[start : start + LANES, :] = best


def body(partial_sums, delays):
    band_count = lax.axis_size("band")
    sections = band_count.bit_length() - 1
    rows, cols = partial_sums.shape
    blocks = cols // LANES
    part = rows // band_count
    counts = right_blocks(band_count)
    params = pltpu.CompilerParams(vmem_limit_bytes=24 * 2**20)

    def struct(*shape, dtype=jnp.float32):
        return jax.ShapeDtypeStruct(shape, dtype)

    packed = pl.pallas_call(
        pack_kernel,
        out_shape=struct(rows * blocks, LANES),
        in_specs=[VMEM],
        out_specs=VMEM,
        compiler_params=params,
    )(partial_sums)
    shifts = pl.pallas_call(
        functools.partial(delays_kernel, sections, band_count, part),
        out_shape=struct(sections, LANES, dtype=jnp.int32),
        in_specs=[VMEM],
        out_specs=VMEM,
        compiler_params=params,
    )(delays)

    mine = lax.all_to_all(packed.reshape(band_count, part * blocks, LANES), "band", split_axis=0, concat_axis=0, tiled=True)
    mine = mine.reshape(rows * blocks, LANES)
    count = lax.axis_size("tm")
    middle_at = count // 2
    wide = sum(counts) * part
    right, left, middle = pl.pallas_call(
        functools.partial(rims_kernel, counts, part, blocks),
        out_shape=[struct(wide, LANES), struct(rows, LANES), struct(wide + 8, LANES)],
        in_specs=[VMEM],
        out_specs=[VMEM] * 3,
        compiler_params=params,
    )(mine)
    middle = lax.ppermute(middle, "tm", [(at - 1, at) for at in (middle_at, middle_at + 1)])
    right = lax.ppermute(right, "tm", [(at, at - 1) for at in range(1, count)])
    left = lax.ppermute(left, "tm", [(at - 1, at) for at in range(1, count) if at not in (middle_at, middle_at + 1)])

    best = pl.pallas_call(
        functools.partial(merge_kernel, sections, counts, part, blocks),
        out_shape=struct(cols, rows),
        in_specs=[SMEM] + [VMEM] * 4,
        out_specs=VMEM,
        scratch_shapes=[pltpu.VMEM((rows * 8, LANES), jnp.float32)] * 4 + [pltpu.VMEM((WMAX + cols, rows), jnp.float32)],
        compiler_params=params,
    )(shifts, mine, right, left, middle)

    slabs = best.reshape(band_count, cols // band_count, rows)
    slabs = lax.all_to_all(slabs, "band", split_axis=0, concat_axis=0, tiled=True)
    return slabs.transpose(1, 0, 2).reshape(cols // band_count, band_count * rows).T


def solution(mesh):
    in_specs = (P("band", "tm"), P())
    out_specs = P(None, ("tm", "band"))
    return jax.shard_map(body, mesh=mesh, in_specs=in_specs, out_specs=out_specs, check_vma=False)
```

```python
import functools
import math

import jax
import jax.numpy as jnp
from jax import lax
from jax.experimental import pallas as pl
from jax.experimental.pallas import tpu as pltpu
from jax.sharding import PartitionSpec as P

HALO = 96
WMAX = 64
LANES = 128
TILE = 8
VMEM = pl.BlockSpec(memory_space=pltpu.VMEM)
SMEM = pl.BlockSpec(memory_space=pltpu.SMEM)


def right_blocks(band_count):
    sections = band_count.bit_length() - 1
    return [-(-HALO * (sections - bin(band).count("1")) // LANES) for band in range(band_count)]


def pack_kernel(x_ref, out_ref):
    rows, cols = x_ref.shape
    blocks = cols // LANES
    for group in range(rows // 8):
        for block in range(blocks):
            out_ref[pl.ds(group * 8 * blocks + block, 8, stride=blocks), :] = x_ref[
                group * 8 : group * 8 + 8, block * LANES : (block + 1) * LANES
            ]


def pick_delays(sections, band_count, part, delays_ref, shifts_ref):
    my_band = lax.axis_index("band")
    lane = lax.broadcasted_iota(jnp.int32, (1, LANES), 1)
    for section_idx in range(sections):
        group = 2 << section_idx
        span = part * group
        first = my_band * span
        line = jnp.zeros((1, LANES), jnp.int32)
        for merged in range(band_count // group):
            column = pl.multiple_of(merged * group * LANES + first // LANES * LANES, LANES)
            values = delays_ref[section_idx : section_idx + 1, pl.ds(column, LANES)]
            turn = lax.rem(merged * span - lax.rem(first, LANES) + LANES, LANES)
            values = pltpu.roll(values, turn, 1)
            line = jnp.where((lane >= merged * span) & (lane < (merged + 1) * span), values, line)
        shifts_ref[section_idx : section_idx + 1, :] = line


def rims_kernel(counts, part, blocks, main_ref, delays_ref, right_ref, left_ref, middle_ref, shifts_ref):
    pick_delays(shifts_ref.shape[0], len(counts), part, delays_ref, shifts_ref)
    rows = len(counts) * part
    place = 0
    for row in range(rows):
        count = counts[row // part]
        if count:
            right_ref[place : place + count, :] = main_ref[row * blocks : row * blocks + count, :]
        place += count
    half = rows // 2
    low = main_ref[pl.ds(blocks - 1, half, stride=blocks), :]
    high = main_ref[pl.ds(half * blocks + blocks - 1, half, stride=blocks), :]
    lane = lax.broadcasted_iota(jnp.int32, (half, LANES), 1)
    both = jnp.where(lane < WMAX, pltpu.roll(low, WMAX, 1), high)
    left_ref[...] = both
    middle_ref[0:half, :] = both


def steps(rows, half):
    for step in range(rows // 2):
        within = step % half
        base = (step - within) * 2
        yield base + within, base + within + half, base + 2 * within


def inner_kernel(sections, band_count, part, blocks, shifts_ref, main_ref, out_ref, tail_ref, firsts_ref, ping, pong, turned):
    rows = band_count * part
    lane = lax.broadcasted_iota(jnp.int32, (TILE, LANES), 1)
    source, target = main_ref, pong
    for section_idx in range(sections):
        for lower, upper, row in steps(rows, part << section_idx):
            low = source[lower * TILE : (lower + 1) * TILE, :]
            later = pltpu.roll(low, TILE - 1, 0)
            up = source[upper * TILE : (upper + 1) * TILE, :]
            for side in range(2):
                at = row + side
                delay = shifts_ref[section_idx, at]
                turn = (LANES - delay) & (LANES - 1)
                merged = up + pltpu.roll(jnp.where(lane >= delay, low, later), turn, 1)
                target[at * TILE : (at + 1) * TILE, :] = merged
                if section_idx < sections - 1:
                    firsts_ref[section_idx * rows + at : section_idx * rows + at + 1, :] = merged[0:1, :]
        source, target = target, ping if section_idx % 2 == 0 else pong

    good = blocks // 2
    for block in range(good):
        turned[block * LANES : (block + 1) * LANES, :] = source[pl.ds(block, rows, stride=TILE), :].T
    tail_ref[0:LANES, :] = turned[0:LANES, :]
    tail_ref[LANES : LANES + WMAX, :] = turned[good * LANES - WMAX : good * LANES, :]
    for block in range(1, good):
        start = block * LANES
        sums = turned[start - WMAX : start + LANES, :]
        out_ref[start : start + LANES, :] = boxcars(sums, band_count)


def boxcars(sums, band_count):
    best = sums[WMAX:, :] * (1.0 / math.sqrt(band_count))
    width = 1
    while width < WMAX:
        sums = sums + pltpu.roll(sums, width, 0)
        width *= 2
        best = jnp.maximum(best, sums[WMAX:, :] * (1.0 / math.sqrt(width * band_count)))
    return best


def outer_kernel(sections, counts, part, blocks, *refs):
    shifts_ref, main_ref, right_ref, left_ref, middle_ref, tail_ref, firsts_ref, inner_ref, out_ref, ping, pong, turned = refs
    del inner_ref
    band_count = len(counts)
    rows = band_count * part
    good = blocks // 2
    lane = lax.broadcasted_iota(jnp.int32, (TILE, LANES), 1)
    slot = lax.broadcasted_iota(jnp.int32, (TILE, LANES), 0)

    places, place = [], 0
    for row in range(rows):
        count = counts[row // part]
        places.append(place)
        ping[row * TILE : row * TILE + good, :] = main_ref[row * blocks + good : (row + 1) * blocks, :]
        kept = min(count, TILE - 1 - good)
        if kept:
            ping[row * TILE + good : row * TILE + good + kept, :] = right_ref[place : place + kept, :]
        place += count

    beyond = lax.axis_index("tm") - lax.axis_size("tm") // 2
    from_left = jnp.where((beyond == 0) | (beyond == 1), middle_ref[0 : rows // 2, :], left_ref[...])
    ping[pl.ds(TILE - 1, rows // 2, stride=TILE), :] = pltpu.roll(from_left, WMAX, 1)
    ping[pl.ds(rows // 2 * TILE + TILE - 1, rows // 2, stride=TILE), :] = from_left

    source, target = ping, pong
    for section_idx in range(sections):
        for lower, upper, row in steps(rows, part << section_idx):
            low = source[lower * TILE : (lower + 1) * TILE, :]
            if section_idx == 0:
                first = main_ref[lower * blocks : lower * blocks + 1, :]
            else:
                at = (section_idx - 1) * rows + lower
                first = firsts_ref[at : at + 1, :]
            later = jnp.where(slot == TILE - 1, first, pltpu.roll(low, TILE - 1, 0))
            if section_idx == 0 and counts[lower // part] == TILE - good:
                fourth = places[lower] + TILE - good - 1
                later = jnp.where(slot == TILE - 2, right_ref[fourth : fourth + 1, :], later)
            up = source[upper * TILE : (upper + 1) * TILE, :]
            for side in range(2):
                at = row + side
                delay = shifts_ref[section_idx, at]
                turn = (LANES - delay) & (LANES - 1)
                target[at * TILE : (at + 1) * TILE, :] = up + pltpu.roll(jnp.where(lane >= delay, low, later), turn, 1)
        source, target = target, source

    before = source[pl.ds(TILE - 1, rows, stride=TILE), :].T[LANES - WMAX :, :]
    before = jnp.where(lax.axis_index("tm") > 0, before, 0.0)
    out_ref[0:LANES, :] = boxcars(jnp.concatenate([before, tail_ref[0:LANES, :]], axis=0), band_count)
    turned[0:WMAX, :] = tail_ref[LANES : LANES + WMAX, :]
    for block in range(blocks - good):
        turned[WMAX + block * LANES : WMAX + (block + 1) * LANES, :] = source[pl.ds(block, rows, stride=TILE), :].T
    for block in range(blocks - good):
        start = block * LANES
        place = (good + block) * LANES
        out_ref[place : place + LANES, :] = boxcars(turned[start : start + LANES + WMAX, :], band_count)


def body(partial_sums, delays):
    band_count = lax.axis_size("band")
    sections = band_count.bit_length() - 1
    rows, cols = partial_sums.shape
    blocks = cols // LANES
    part = rows // band_count
    counts = right_blocks(band_count)
    params = pltpu.CompilerParams(vmem_limit_bytes=24 * 2**20)

    def struct(*shape, dtype=jnp.float32):
        return jax.ShapeDtypeStruct(shape, dtype)

    def scratch(*shape):
        return pltpu.VMEM(shape, jnp.float32)

    packed = pl.pallas_call(
        pack_kernel,
        out_shape=struct(rows * blocks, LANES),
        in_specs=[VMEM],
        out_specs=VMEM,
        compiler_params=params,
    )(partial_sums)
    mine = lax.all_to_all(packed.reshape(band_count, part * blocks, LANES), "band", split_axis=0, concat_axis=0, tiled=True)
    mine = mine.reshape(rows * blocks, LANES)

    count = lax.axis_size("tm")
    middle_at = count // 2
    wide = sum(counts) * part
    right, left, middle, shifts = pl.pallas_call(
        functools.partial(rims_kernel, counts, part, blocks),
        out_shape=[
            struct(wide, LANES),
            struct(rows // 2, LANES),
            struct(wide + TILE, LANES),
            struct(sections, LANES, dtype=jnp.int32),
        ],
        in_specs=[VMEM] * 2,
        out_specs=[VMEM] * 4,
        compiler_params=params,
    )(mine, delays)

    middle = lax.ppermute(middle, "tm", [(at - 1, at) for at in (middle_at, middle_at + 1)])
    right = lax.ppermute(right, "tm", [(at, at - 1) for at in range(1, count)])
    left = lax.ppermute(left, "tm", [(at - 1, at) for at in range(1, count) if at not in (middle_at, middle_at + 1)])

    inner, tail, firsts = pl.pallas_call(
        functools.partial(inner_kernel, sections, band_count, part, blocks),
        out_shape=[struct(cols, rows), struct(LANES + WMAX, rows), struct((sections - 1) * rows, LANES)],
        in_specs=[SMEM, VMEM],
        out_specs=[VMEM] * 3,
        scratch_shapes=[scratch(rows * TILE, LANES), scratch(rows * TILE, LANES), scratch(cols // 2, rows)],
        compiler_params=params,
        cost_estimate=pl.CostEstimate(flops=2 * 10**6, bytes_accessed=4 * 2**20, transcendentals=0),
    )(shifts, mine)
    best = pl.pallas_call(
        functools.partial(outer_kernel, sections, counts, part, blocks),
        out_shape=struct(cols, rows),
        in_specs=[SMEM] + [VMEM] * 7,
        out_specs=VMEM,
        scratch_shapes=[scratch(rows * TILE, LANES), scratch(rows * TILE, LANES), scratch(WMAX + cols // 2, rows)],
        compiler_params=params,
        input_output_aliases={7: 0},
    )(shifts, mine, right, left, middle, tail, firsts, inner)

    slabs = best.reshape(band_count, cols // band_count, rows)
    slabs = lax.all_to_all(slabs, "band", split_axis=0, concat_axis=0, tiled=True)
    return slabs.transpose(1, 0, 2).reshape(cols // band_count, band_count * rows).T


def solution(mesh):
    in_specs = (P("band", "tm"), P())
    out_specs = P(None, ("tm", "band"))
    return jax.shard_map(body, mesh=mesh, in_specs=in_specs, out_specs=out_specs, check_vma=False)
```

```python
import functools
import math

import jax
import jax.numpy as jnp
from jax import lax
from jax.experimental import pallas as pl
from jax.experimental.pallas import tpu as pltpu
from jax.sharding import PartitionSpec as P

HALO = 96
WMAX = 64
LANES = 128
TILE = 8
VMEM = pl.BlockSpec(memory_space=pltpu.VMEM)


def right_blocks(band_count):
    sections = band_count.bit_length() - 1
    widths = [HALO * (sections - bin(band).count("1")) for band in range(band_count)]
    return [
        (width // LANES, width % LANES) if width % LANES <= LANES // 2 else (width // LANES + 1, 0) for width in widths
    ]


def right_rows(counts, part):
    return sum(whole * part + left_over * part // LANES for whole, left_over in counts)


def pack_kernel(x_ref, out_ref):
    rows, cols = x_ref.shape
    blocks = cols // LANES
    for group in range(rows // 8):
        for block in range(blocks):
            out_ref[pl.ds(group * 8 * blocks + block, 8, stride=blocks), :] = x_ref[
                group * 8 : group * 8 + 8, block * LANES : (block + 1) * LANES
            ]


def pick_delays(sections, band_count, part, delays_ref, shifts_ref):
    my_band = lax.axis_index("band")
    lane = lax.broadcasted_iota(jnp.int32, (1, LANES), 1)
    for section_idx in range(sections):
        group = 2 << section_idx
        span = part * group
        first = my_band * span
        line = jnp.zeros((1, LANES), jnp.int32)
        for merged in range(band_count // group):
            column = pl.multiple_of(merged * group * LANES + first // LANES * LANES, LANES)
            values = delays_ref[section_idx : section_idx + 1, pl.ds(column, LANES)]
            turn = lax.rem(merged * span - lax.rem(first, LANES) + LANES, LANES)
            values = pltpu.roll(values, turn, 1)
            line = jnp.where((lane >= merged * span) & (lane < (merged + 1) * span), values, line)
        shifts_ref[section_idx : section_idx + 1, :] = line


def rims_kernel(counts, part, blocks, main_ref, delays_ref, right_ref, left_ref, middle_ref, shifts_ref):
    pick_delays(shifts_ref.shape[0], len(counts), part, delays_ref, shifts_ref)
    rows = len(counts) * part
    one = lax.broadcasted_iota(jnp.int32, (1, LANES), 1)
    place = 0
    for band, (count, over) in enumerate(counts):
        for row in range(band * part, (band + 1) * part):
            if count:
                right_ref[place : place + count, :] = main_ref[row * blocks : row * blocks + count, :]
            place += count
        share = LANES // over if over else part
        for first in range(band * part, (band + 1) * part, share) if over else ():
            line = main_ref[first * blocks + count : first * blocks + count + 1, :]
            for index in range(1, share):
                start = (first + index) * blocks + count
                piece = pltpu.roll(main_ref[start : start + 1, :], index * over, 1)
                line = jnp.where(one < index * over, line, piece)
            right_ref[place : place + 1, :] = line
            place += 1
    half = rows // 2
    low = main_ref[pl.ds(blocks - 1, half, stride=blocks), :]
    high = main_ref[pl.ds(half * blocks + blocks - 1, half, stride=blocks), :]
    lane = lax.broadcasted_iota(jnp.int32, (half, LANES), 1)
    both = jnp.where(lane < WMAX, pltpu.roll(low, WMAX, 1), high)
    left_ref[...] = both
    middle_ref[0:half, :] = both


def steps(rows, half):
    for step in range(rows // 2):
        within = step % half
        base = (step - within) * 2
        yield base + within, base + within + half, base + 2 * within


def inner_kernel(sections, band_count, part, blocks, table_ref, main_ref, out_ref, tail_ref, firsts_ref, outer_ref, *scratch):
    ping, pong, turned, shifts_ref, sem = scratch
    copy = pltpu.make_async_copy(table_ref, shifts_ref, sem)
    copy.start()
    rows = band_count * part
    good = blocks // 2
    lane = lax.broadcasted_iota(jnp.int32, (TILE, LANES), 1)
    for row in range(rows):
        outer_ref[row * TILE : row * TILE + good, :] = main_ref[row * blocks + good : (row + 1) * blocks, :]
    copy.wait()

    source, target = main_ref, pong
    for section_idx in range(sections):
        for lower, upper, row in steps(rows, part << section_idx):
            low = source[lower * TILE : (lower + 1) * TILE, :]
            later = source[lower * TILE + 1 : (lower + 1) * TILE + 1, :]
            up = source[upper * TILE : (upper + 1) * TILE, :]
            for side in range(2):
                at = row + side
                delay = shifts_ref[section_idx, at]
                turn = (LANES - delay) & (LANES - 1)
                merged = up + pltpu.roll(jnp.where(lane >= delay, low, later), turn, 1)
                target[at * TILE : (at + 1) * TILE, :] = merged
                if section_idx < sections - 1:
                    firsts_ref[section_idx * rows + at : section_idx * rows + at + 1, :] = merged[0:1, :]
        source, target = target, ping if section_idx % 2 == 0 else pong

    for block in range(good):
        turned[block * LANES : (block + 1) * LANES, :] = source[pl.ds(block, rows, stride=TILE), :].T
    tail_ref[0:LANES, :] = turned[0:LANES, :]
    tail_ref[LANES : LANES + WMAX, :] = turned[good * LANES - WMAX : good * LANES, :]
    for block in range(1, good):
        start = block * LANES
        sums = turned[start - WMAX : start + LANES, :]
        out_ref[start : start + LANES, :] = boxcars(sums, band_count)


def boxcars(sums, band_count):
    best = sums[WMAX:, :] * (1.0 / math.sqrt(band_count))
    width = 1
    while width < WMAX:
        sums = sums + pltpu.roll(sums, width, 0)
        width *= 2
        best = jnp.maximum(best, sums[WMAX:, :] * (1.0 / math.sqrt(width * band_count)))
    return best


def outer_kernel(sections, counts, part, blocks, *refs):
    table_ref, main_ref, right_ref, left_ref, middle_ref, tail_ref, firsts_ref = refs[:7]
    out_ref, ping, pong, turned, shifts_ref, sem = refs[9:]
    copy = pltpu.make_async_copy(table_ref, shifts_ref, sem)
    copy.start()
    band_count = len(counts)
    rows = band_count * part
    good = blocks // 2
    lane = lax.broadcasted_iota(jnp.int32, (TILE, LANES), 1)
    slot = lax.broadcasted_iota(jnp.int32, (TILE, LANES), 0)

    places, place = [], 0
    for band, (count, over) in enumerate(counts):
        kept = min(count, TILE - 1 - good)
        for row in range(band * part, (band + 1) * part):
            places.append(place)
            if kept:
                ping[row * TILE + good : row * TILE + good + kept, :] = right_ref[place : place + kept, :]
            place += count
        share = LANES // over if over else part
        for row in range(band * part, (band + 1) * part) if over else ():
            index = row % share
            line = right_ref[place : place + 1, :]
            if index:
                line = pltpu.roll(line, LANES - index * over, 1)
            ping[row * TILE + good + count : row * TILE + good + count + 1, :] = line
            place += index == share - 1

    beyond = lax.axis_index("tm") - lax.axis_size("tm") // 2
    from_left = jnp.where((beyond == 0) | (beyond == 1), middle_ref[0 : rows // 2, :], left_ref[...])
    ping[pl.ds(TILE - 1, rows // 2, stride=TILE), :] = pltpu.roll(from_left, WMAX, 1)
    ping[pl.ds(rows // 2 * TILE + TILE - 1, rows // 2, stride=TILE), :] = from_left
    copy.wait()

    source, target = ping, pong
    for section_idx in range(sections):
        for lower, upper, row in steps(rows, part << section_idx):
            low = source[lower * TILE : (lower + 1) * TILE, :]
            if section_idx == 0:
                first = main_ref[lower * blocks : lower * blocks + 1, :]
            else:
                at = (section_idx - 1) * rows + lower
                first = firsts_ref[at : at + 1, :]
            later = jnp.where(slot == TILE - 1, first, source[lower * TILE + 1 : (lower + 1) * TILE + 1, :])
            if section_idx == 0 and counts[lower // part][0] == TILE - good:
                fourth = places[lower] + TILE - good - 1
                later = jnp.where(slot == TILE - 2, right_ref[fourth : fourth + 1, :], later)
            up = source[upper * TILE : (upper + 1) * TILE, :]
            for side in range(2):
                at = row + side
                delay = shifts_ref[section_idx, at]
                turn = (LANES - delay) & (LANES - 1)
                target[at * TILE : (at + 1) * TILE, :] = up + pltpu.roll(jnp.where(lane >= delay, low, later), turn, 1)
        source, target = target, source

    before = source[pl.ds(TILE - 1, rows, stride=TILE), :].T[LANES - WMAX :, :]
    before = jnp.where(lax.axis_index("tm") > 0, before, 0.0)
    out_ref[0:LANES, :] = boxcars(jnp.concatenate([before, tail_ref[0:LANES, :]], axis=0), band_count)
    turned[0:WMAX, :] = tail_ref[LANES : LANES + WMAX, :]
    for block in range(blocks - good):
        turned[WMAX + block * LANES : WMAX + (block + 1) * LANES, :] = source[pl.ds(block, rows, stride=TILE), :].T
    for block in range(blocks - good):
        start = block * LANES
        place = (good + block) * LANES
        out_ref[place : place + LANES, :] = boxcars(turned[start : start + LANES + WMAX, :], band_count)


def body(partial_sums, delays):
    band_count = lax.axis_size("band")
    sections = band_count.bit_length() - 1
    rows, cols = partial_sums.shape
    blocks = cols // LANES
    part = rows // band_count
    counts = right_blocks(band_count)
    params = pltpu.CompilerParams(vmem_limit_bytes=24 * 2**20)

    def struct(*shape, dtype=jnp.float32):
        return jax.ShapeDtypeStruct(shape, dtype)

    def scratch(*shape):
        return pltpu.VMEM(shape, jnp.float32)

    table = pltpu.SMEM((sections, LANES), jnp.int32)

    packed = pl.pallas_call(
        pack_kernel,
        out_shape=struct(rows * blocks, LANES),
        in_specs=[VMEM],
        out_specs=VMEM,
        compiler_params=params,
    )(partial_sums)
    mine = lax.all_to_all(packed.reshape(band_count, part * blocks, LANES), "band", split_axis=0, concat_axis=0, tiled=True)
    mine = mine.reshape(rows * blocks, LANES)

    count = lax.axis_size("tm")
    middle_at = count // 2
    wide = -(-right_rows(counts, part) // TILE) * TILE
    right, left, middle, shifts = pl.pallas_call(
        functools.partial(rims_kernel, counts, part, blocks),
        out_shape=[
            struct(wide, LANES),
            struct(rows // 2, LANES),
            struct(wide + TILE, LANES),
            struct(sections, LANES, dtype=jnp.int32),
        ],
        in_specs=[VMEM] * 2,
        out_specs=[VMEM] * 4,
        compiler_params=params,
    )(mine, delays)

    middle = lax.ppermute(middle, "tm", [(at - 1, at) for at in (middle_at, middle_at + 1)])
    right = lax.ppermute(right, "tm", [(at, at - 1) for at in range(1, count)])
    left = lax.ppermute(left, "tm", [(at - 1, at) for at in range(1, count) if at not in (middle_at, middle_at + 1)])

    merge_scratch = [scratch(rows * TILE, LANES), scratch(WMAX + cols // 2, rows), table, pltpu.SemaphoreType.DMA(())]
    tile_rows = struct(rows * TILE, LANES)
    inner, tail, firsts, outer = pl.pallas_call(
        functools.partial(inner_kernel, sections, band_count, part, blocks),
        out_shape=[struct(cols, rows), struct(LANES + WMAX, rows), struct((sections - 1) * rows, LANES), tile_rows],
        in_specs=[VMEM] * 2,
        out_specs=[VMEM] * 4,
        scratch_shapes=[scratch(rows * TILE, LANES)] + merge_scratch,
        compiler_params=params,
        cost_estimate=pl.CostEstimate(flops=2 * 10**6, bytes_accessed=4 * 2**20, transcendentals=0),
    )(shifts, mine)
    best, _ = pl.pallas_call(
        functools.partial(outer_kernel, sections, counts, part, blocks),
        out_shape=[struct(cols, rows), tile_rows],
        in_specs=[VMEM] * 9,
        out_specs=[VMEM] * 2,
        scratch_shapes=merge_scratch,
        compiler_params=params,
        input_output_aliases={7: 0, 8: 1},
    )(shifts, mine, right, left, middle, tail, firsts, inner, outer)

    slabs = best.reshape(band_count, cols // band_count, rows)
    slabs = lax.all_to_all(slabs, "band", split_axis=0, concat_axis=0, tiled=True)
    return slabs.transpose(1, 0, 2).reshape(cols // band_count, band_count * rows).T


def solution(mesh):
    in_specs = (P("band", "tm"), P())
    out_specs = P(None, ("tm", "band"))
    return jax.shard_map(body, mesh=mesh, in_specs=in_specs, out_specs=out_specs, check_vma=False)
```

```python
import functools
import math

import jax
import jax.numpy as jnp
from jax import lax
from jax.experimental import pallas as pl
from jax.experimental.pallas import tpu as pltpu
from jax.sharding import PartitionSpec as P

HALO = 96
WMAX = 64
LANES = 128
TILE = 8
VMEM = pl.BlockSpec(memory_space=pltpu.VMEM)


def right_blocks(band_count):
    sections = band_count.bit_length() - 1
    widths = [HALO * (sections - bin(band).count("1")) for band in range(band_count)]
    return [
        (width // LANES, width % LANES) if width % LANES <= LANES // 2 else (width // LANES + 1, 0) for width in widths
    ]


def right_rows(counts, part):
    return sum(whole * part + left_over * part // LANES for whole, left_over in counts)


def pack_kernel(x_ref, out_ref):
    rows, cols = x_ref.shape
    blocks = cols // LANES
    for group in range(rows // 8):
        for block in range(blocks):
            out_ref[pl.ds(group * 8 * blocks + block, 8, stride=blocks), :] = x_ref[
                group * 8 : group * 8 + 8, block * LANES : (block + 1) * LANES
            ]


def pick_delays(sections, band_count, part, delays_ref, shifts_ref):
    my_band = lax.axis_index("band")
    lane = lax.broadcasted_iota(jnp.int32, (1, LANES), 1)
    for section_idx in range(sections):
        group = 2 << section_idx
        span = part * group
        first = my_band * span
        line = jnp.zeros((1, LANES), jnp.int32)
        for merged in range(band_count // group):
            column = pl.multiple_of(merged * group * LANES + first // LANES * LANES, LANES)
            values = delays_ref[section_idx : section_idx + 1, pl.ds(column, LANES)]
            turn = lax.rem(merged * span - lax.rem(first, LANES) + LANES, LANES)
            values = pltpu.roll(values, turn, 1)
            line = jnp.where((lane >= merged * span) & (lane < (merged + 1) * span), values, line)
        shifts_ref[section_idx : section_idx + 1, :] = line


def rims_kernel(counts, part, blocks, main_ref, delays_ref, right_ref, left_ref, middle_ref, shifts_ref):
    pick_delays(shifts_ref.shape[0], len(counts), part, delays_ref, shifts_ref)
    rows = len(counts) * part
    one = lax.broadcasted_iota(jnp.int32, (1, LANES), 1)
    place = 0
    for band, (count, over) in enumerate(counts):
        for row in range(band * part, (band + 1) * part):
            if count:
                right_ref[place : place + count, :] = main_ref[row * blocks : row * blocks + count, :]
            place += count
        share = LANES // over if over else part
        for first in range(band * part, (band + 1) * part, share) if over else ():
            line = main_ref[first * blocks + count : first * blocks + count + 1, :]
            for index in range(1, share):
                start = (first + index) * blocks + count
                piece = pltpu.roll(main_ref[start : start + 1, :], index * over, 1)
                line = jnp.where(one < index * over, line, piece)
            right_ref[place : place + 1, :] = line
            place += 1
    half = rows // 2
    low = main_ref[pl.ds(blocks - 1, half, stride=blocks), :]
    high = main_ref[pl.ds(half * blocks + blocks - 1, half, stride=blocks), :]
    lane = lax.broadcasted_iota(jnp.int32, (half, LANES), 1)
    both = jnp.where(lane < WMAX, pltpu.roll(low, WMAX, 1), high)
    left_ref[...] = both
    middle_ref[0:half, :] = both


def steps(rows, half):
    for step in range(rows // 2):
        within = step % half
        base = (step - within) * 2
        yield base + within, base + within + half, base + 2 * within


def inner_kernel(sections, band_count, part, blocks, table_ref, main_ref, out_ref, tail_ref, firsts_ref, outer_ref, *scratch):
    ping, pong, turned, shifts_ref, sem = scratch
    copy = pltpu.make_async_copy(table_ref, shifts_ref, sem)
    copy.start()
    rows = band_count * part
    good = blocks // 2
    lane = lax.broadcasted_iota(jnp.int32, (TILE, LANES), 1)
    for row in range(rows):
        outer_ref[row * TILE : row * TILE + good, :] = main_ref[row * blocks + good : (row + 1) * blocks, :]
    copy.wait()

    source, target = main_ref, pong
    for section_idx in range(sections):
        for lower, upper, row in steps(rows, part << section_idx):
            low = source[lower * TILE : (lower + 1) * TILE, :]
            later = source[lower * TILE + 1 : (lower + 1) * TILE + 1, :]
            up = source[upper * TILE : (upper + 1) * TILE, :]
            for side in range(2):
                at = row + side
                delay = shifts_ref[section_idx, at]
                turn = (LANES - delay) & (LANES - 1)
                merged = up + pltpu.roll(jnp.where(lane >= delay, low, later), turn, 1)
                target[at * TILE : (at + 1) * TILE, :] = merged
                if section_idx < sections - 1:
                    firsts_ref[section_idx * rows + at : section_idx * rows + at + 1, :] = merged[0:1, :]
        source, target = target, ping if section_idx % 2 == 0 else pong

    for block in range(good):
        turned[block * LANES : (block + 1) * LANES, :] = source[pl.ds(block, rows, stride=TILE), :].T
    tail_ref[0:LANES, :] = turned[0:LANES, :]
    tail_ref[LANES : LANES + WMAX, :] = turned[good * LANES - WMAX : good * LANES, :]
    for block in range(1, good):
        start = block * LANES
        sums = turned[start - WMAX : start + LANES, :]
        out_ref[start - LANES : start, :] = boxcars(sums, band_count)


def boxcars(sums, band_count):
    best = sums[WMAX:, :] * (1.0 / math.sqrt(band_count))
    width = 1
    while width < WMAX:
        sums = sums + pltpu.roll(sums, width, 0)
        width *= 2
        best = jnp.maximum(best, sums[WMAX:, :] * (1.0 / math.sqrt(width * band_count)))
    return best


def outer_kernel(sections, counts, part, blocks, *refs):
    table_ref, main_ref, right_ref, left_ref, middle_ref, tail_ref, firsts_ref, inner_ref, outer_ref = refs[:9]
    out_ref, ping, pong, turned, shifts_ref, sem = refs[9:]
    copy = pltpu.make_async_copy(table_ref, shifts_ref, sem)
    copy.start()
    out_ref[LANES : LANES + inner_ref.shape[0], :] = inner_ref[...]
    ping[...] = outer_ref[...]
    band_count = len(counts)
    rows = band_count * part
    good = blocks // 2
    lane = lax.broadcasted_iota(jnp.int32, (TILE, LANES), 1)
    slot = lax.broadcasted_iota(jnp.int32, (TILE, LANES), 0)

    places, place = [], 0
    for band, (count, over) in enumerate(counts):
        kept = min(count, TILE - 1 - good)
        for row in range(band * part, (band + 1) * part):
            places.append(place)
            if kept:
                ping[row * TILE + good : row * TILE + good + kept, :] = right_ref[place : place + kept, :]
            place += count
        share = LANES // over if over else part
        for row in range(band * part, (band + 1) * part) if over else ():
            index = row % share
            line = right_ref[place : place + 1, :]
            if index:
                line = pltpu.roll(line, LANES - index * over, 1)
            ping[row * TILE + good + count : row * TILE + good + count + 1, :] = line
            place += index == share - 1

    beyond = lax.axis_index("tm") - lax.axis_size("tm") // 2
    from_left = jnp.where((beyond == 0) | (beyond == 1), middle_ref[0 : rows // 2, :], left_ref[...])
    ping[pl.ds(TILE - 1, rows // 2, stride=TILE), :] = pltpu.roll(from_left, WMAX, 1)
    ping[pl.ds(rows // 2 * TILE + TILE - 1, rows // 2, stride=TILE), :] = from_left
    copy.wait()

    source, target = ping, pong
    for section_idx in range(sections):
        for lower, upper, row in steps(rows, part << section_idx):
            low = source[lower * TILE : (lower + 1) * TILE, :]
            if section_idx == 0:
                first = main_ref[lower * blocks : lower * blocks + 1, :]
            else:
                at = (section_idx - 1) * rows + lower
                first = firsts_ref[at : at + 1, :]
            later = jnp.where(slot == TILE - 1, first, source[lower * TILE + 1 : (lower + 1) * TILE + 1, :])
            if section_idx == 0 and counts[lower // part][0] == TILE - good:
                fourth = places[lower] + TILE - good - 1
                later = jnp.where(slot == TILE - 2, right_ref[fourth : fourth + 1, :], later)
            up = source[upper * TILE : (upper + 1) * TILE, :]
            for side in range(2):
                at = row + side
                delay = shifts_ref[section_idx, at]
                turn = (LANES - delay) & (LANES - 1)
                target[at * TILE : (at + 1) * TILE, :] = up + pltpu.roll(jnp.where(lane >= delay, low, later), turn, 1)
        source, target = target, source

    before = source[pl.ds(TILE - 1, rows, stride=TILE), :].T[LANES - WMAX :, :]
    before = jnp.where(lax.axis_index("tm") > 0, before, 0.0)
    out_ref[0:LANES, :] = boxcars(jnp.concatenate([before, tail_ref[0:LANES, :]], axis=0), band_count)
    turned[0:WMAX, :] = tail_ref[LANES : LANES + WMAX, :]
    for block in range(blocks - good):
        turned[WMAX + block * LANES : WMAX + (block + 1) * LANES, :] = source[pl.ds(block, rows, stride=TILE), :].T
    for block in range(blocks - good):
        start = block * LANES
        place = (good + block) * LANES
        out_ref[place : place + LANES, :] = boxcars(turned[start : start + LANES + WMAX, :], band_count)


def body(partial_sums, delays):
    band_count = lax.axis_size("band")
    sections = band_count.bit_length() - 1
    rows, cols = partial_sums.shape
    blocks = cols // LANES
    part = rows // band_count
    counts = right_blocks(band_count)
    params = pltpu.CompilerParams(vmem_limit_bytes=24 * 2**20)

    def struct(*shape, dtype=jnp.float32):
        return jax.ShapeDtypeStruct(shape, dtype)

    def scratch(*shape):
        return pltpu.VMEM(shape, jnp.float32)

    table = pltpu.SMEM((sections, LANES), jnp.int32)

    packed = pl.pallas_call(
        pack_kernel,
        out_shape=struct(rows * blocks, LANES),
        in_specs=[VMEM],
        out_specs=VMEM,
        compiler_params=params,
    )(partial_sums)
    mine = lax.all_to_all(packed.reshape(band_count, part * blocks, LANES), "band", split_axis=0, concat_axis=0, tiled=True)
    mine = mine.reshape(rows * blocks, LANES)

    count = lax.axis_size("tm")
    middle_at = count // 2
    wide = -(-right_rows(counts, part) // TILE) * TILE
    right, left, middle, shifts = pl.pallas_call(
        functools.partial(rims_kernel, counts, part, blocks),
        out_shape=[
            struct(wide, LANES),
            struct(rows // 2, LANES),
            struct(wide + TILE, LANES),
            struct(sections, LANES, dtype=jnp.int32),
        ],
        in_specs=[VMEM] * 2,
        out_specs=[VMEM] * 4,
        compiler_params=params,
    )(mine, delays)

    middle = lax.ppermute(middle, "tm", [(at - 1, at) for at in (middle_at, middle_at + 1)])
    right = lax.ppermute(right, "tm", [(at, at - 1) for at in range(1, count)])
    left = lax.ppermute(left, "tm", [(at - 1, at) for at in range(1, count) if at not in (middle_at, middle_at + 1)])

    merge_scratch = [scratch(rows * TILE, LANES), scratch(WMAX + cols // 2, rows), table, pltpu.SemaphoreType.DMA(())]
    tile_rows = struct(rows * TILE, LANES)
    inner, tail, firsts, outer = pl.pallas_call(
        functools.partial(inner_kernel, sections, band_count, part, blocks),
        out_shape=[
            struct(cols // 2 - LANES, rows),
            struct(LANES + WMAX, rows),
            struct((sections - 1) * rows, LANES),
            tile_rows,
        ],
        in_specs=[VMEM] * 2,
        out_specs=[VMEM] * 4,
        scratch_shapes=[scratch(rows * TILE, LANES)] + merge_scratch,
        compiler_params=params,
        cost_estimate=pl.CostEstimate(flops=2 * 10**6, bytes_accessed=4 * 2**20, transcendentals=0),
    )(shifts, mine)
    best = pl.pallas_call(
        functools.partial(outer_kernel, sections, counts, part, blocks),
        out_shape=struct(cols, rows),
        in_specs=[VMEM] * 9,
        out_specs=VMEM,
        scratch_shapes=[scratch(rows * TILE, LANES)] + merge_scratch,
        compiler_params=params,
    )(shifts, mine, right, left, middle, tail, firsts, inner, outer)

    slabs = best.reshape(band_count, cols // band_count, rows)
    slabs = lax.all_to_all(slabs, "band", split_axis=0, concat_axis=0, tiled=True)
    return slabs.transpose(1, 0, 2).reshape(cols // band_count, band_count * rows).T


def solution(mesh):
    in_specs = (P("band", "tm"), P())
    out_specs = P(None, ("tm", "band"))
    return jax.shard_map(body, mesh=mesh, in_specs=in_specs, out_specs=out_specs, check_vma=False)
```

```python
import functools
import math

import jax
import jax.numpy as jnp
from jax import lax
from jax.experimental import pallas as pl
from jax.experimental.pallas import tpu as pltpu
from jax.sharding import PartitionSpec as P

HALO = 96
WMAX = 64
LANES = 128
TILE = 8
VMEM = pl.BlockSpec(memory_space=pltpu.VMEM)


def right_blocks(band_count):
    sections = band_count.bit_length() - 1
    widths = [HALO * (sections - bin(band).count("1")) for band in range(band_count)]
    return [
        (width // LANES, width % LANES) if width % LANES <= LANES // 2 else (width // LANES + 1, 0) for width in widths
    ]


def right_rows(counts, part):
    return sum(whole * part + left_over * part // LANES for whole, left_over in counts)


def pack_kernel(x_ref, out_ref):
    rows, cols = x_ref.shape
    blocks = cols // LANES
    for group in range(rows // 8):
        for block in range(blocks):
            out_ref[pl.ds(group * 8 * blocks + block, 8, stride=blocks), :] = x_ref[
                group * 8 : group * 8 + 8, block * LANES : (block + 1) * LANES
            ]


def pick_delays(sections, band_count, part, delays_ref, shifts_ref):
    my_band = lax.axis_index("band")
    lane = lax.broadcasted_iota(jnp.int32, (1, LANES), 1)
    for section_idx in range(sections):
        group = 2 << section_idx
        span = part * group
        first = my_band * span
        line = jnp.zeros((1, LANES), jnp.int32)
        for merged in range(band_count // group):
            column = pl.multiple_of(merged * group * LANES + first // LANES * LANES, LANES)
            values = delays_ref[section_idx : section_idx + 1, pl.ds(column, LANES)]
            turn = lax.rem(merged * span - lax.rem(first, LANES) + LANES, LANES)
            values = pltpu.roll(values, turn, 1)
            line = jnp.where((lane >= merged * span) & (lane < (merged + 1) * span), values, line)
        shifts_ref[section_idx : section_idx + 1, :] = line


def rims_kernel(counts, part, blocks, main_ref, delays_ref, right_ref, left_ref, middle_ref, shifts_ref):
    pick_delays(shifts_ref.shape[0], len(counts), part, delays_ref, shifts_ref)
    rows = len(counts) * part
    one = lax.broadcasted_iota(jnp.int32, (1, LANES), 1)
    place = 0
    for band, (count, over) in enumerate(counts):
        for row in range(band * part, (band + 1) * part):
            if count:
                right_ref[place : place + count, :] = main_ref[row * blocks : row * blocks + count, :]
            place += count
        share = LANES // over if over else part
        for first in range(band * part, (band + 1) * part, share) if over else ():
            line = main_ref[first * blocks + count : first * blocks + count + 1, :]
            for index in range(1, share):
                start = (first + index) * blocks + count
                piece = pltpu.roll(main_ref[start : start + 1, :], index * over, 1)
                line = jnp.where(one < index * over, line, piece)
            right_ref[place : place + 1, :] = line
            place += 1
    half = rows // 2
    low = main_ref[pl.ds(blocks - 1, half, stride=blocks), :]
    high = main_ref[pl.ds(half * blocks + blocks - 1, half, stride=blocks), :]
    lane = lax.broadcasted_iota(jnp.int32, (half, LANES), 1)
    both = jnp.where(lane < WMAX, pltpu.roll(low, WMAX, 1), high)
    left_ref[...] = both
    middle_ref[0:half, :] = both


def steps(rows, half):
    for step in range(rows // 2):
        within = step % half
        base = (step - within) * 2
        yield base + within, base + within + half, base + 2 * within


def inner_kernel(sections, band_count, part, blocks, table_ref, main_ref, out_ref, tail_ref, firsts_ref, outer_ref, *scratch):
    ping, pong, turned, shifts_ref, sem = scratch
    copy = pltpu.make_async_copy(table_ref, shifts_ref, sem)
    copy.start()
    rows = band_count * part
    good = blocks // 2
    lane = lax.broadcasted_iota(jnp.int32, (TILE, LANES), 1)
    for row in range(rows):
        outer_ref[row * TILE : row * TILE + good, :] = main_ref[row * blocks + good : (row + 1) * blocks, :]
    copy.wait()

    source, target = main_ref, pong
    for section_idx in range(sections):
        for lower, upper, row in steps(rows, part << section_idx):
            low = source[lower * TILE : (lower + 1) * TILE, :]
            later = source[lower * TILE + 1 : (lower + 1) * TILE + 1, :]
            up = source[upper * TILE : (upper + 1) * TILE, :]
            for side in range(2):
                at = row + side
                delay = shifts_ref[section_idx, at]
                turn = (LANES - delay) & (LANES - 1)
                merged = up + pltpu.roll(jnp.where(lane >= delay, low, later), turn, 1)
                target[at * TILE : (at + 1) * TILE, :] = merged
                if section_idx < sections - 1:
                    firsts_ref[section_idx * rows + at : section_idx * rows + at + 1, :] = merged[0:1, :]
        source, target = target, ping if section_idx % 2 == 0 else pong

    for block in range(good):
        turned[block * LANES : (block + 1) * LANES, :] = source[pl.ds(block, rows, stride=TILE), :].T
    tail_ref[0:LANES, :] = turned[0:LANES, :]
    tail_ref[LANES : LANES + WMAX, :] = turned[good * LANES - WMAX : good * LANES, :]
    stream(turned, LANES, (good - 1) * LANES, out_ref, 0, band_count)


def boxcars(sums, band_count):
    best = sums[WMAX:, :] * (1.0 / math.sqrt(band_count))
    width = 1
    while width < WMAX:
        sums = sums + pltpu.roll(sums, width, 0)
        width *= 2
        best = jnp.maximum(best, sums[WMAX:, :] * (1.0 / math.sqrt(width * band_count)))
    return best


def stream(turned, start, length, out_ref, place, band_count):
    index = lax.broadcasted_iota(jnp.int32, (TILE, LANES), 0)
    turns, past = {}, []
    for at in range(start - WMAX, start + length, TILE):
        sums = turned[at : at + TILE, :]
        best = sums * (1.0 / math.sqrt(band_count))
        held = {}
        width = 1
        while width < WMAX:
            held[width] = sums
            if width < TILE:
                turn = pltpu.roll(sums, width, 0)
                earlier = jnp.where(index < width, turns.get(width, turn), turn)
                turns[width] = turn
            else:
                back = width // TILE
                earlier = past[-back][width] if len(past) >= back else sums
            sums = sums + earlier
            width *= 2
            best = jnp.maximum(best, sums * (1.0 / math.sqrt(width * band_count)))
        past.append(held)
        if at >= start:
            out_ref[place + at - start : place + at - start + TILE, :] = best


def outer_kernel(sections, counts, part, blocks, *refs):
    table_ref, main_ref, right_ref, left_ref, middle_ref, tail_ref, firsts_ref, inner_ref, outer_ref = refs[:9]
    out_ref, ping, pong, turned, shifts_ref, sem = refs[9:]
    copy = pltpu.make_async_copy(table_ref, shifts_ref, sem)
    copy.start()
    out_ref[LANES : LANES + inner_ref.shape[0], :] = inner_ref[...]
    ping[...] = outer_ref[...]
    band_count = len(counts)
    rows = band_count * part
    good = blocks // 2
    lane = lax.broadcasted_iota(jnp.int32, (TILE, LANES), 1)
    slot = lax.broadcasted_iota(jnp.int32, (TILE, LANES), 0)

    places, place = [], 0
    for band, (count, over) in enumerate(counts):
        kept = min(count, TILE - 1 - good)
        for row in range(band * part, (band + 1) * part):
            places.append(place)
            if kept:
                ping[row * TILE + good : row * TILE + good + kept, :] = right_ref[place : place + kept, :]
            place += count
        share = LANES // over if over else part
        for row in range(band * part, (band + 1) * part) if over else ():
            index = row % share
            line = right_ref[place : place + 1, :]
            if index:
                line = pltpu.roll(line, LANES - index * over, 1)
            ping[row * TILE + good + count : row * TILE + good + count + 1, :] = line
            place += index == share - 1

    beyond = lax.axis_index("tm") - lax.axis_size("tm") // 2
    from_left = jnp.where((beyond == 0) | (beyond == 1), middle_ref[0 : rows // 2, :], left_ref[...])
    ping[pl.ds(TILE - 1, rows // 2, stride=TILE), :] = pltpu.roll(from_left, WMAX, 1)
    ping[pl.ds(rows // 2 * TILE + TILE - 1, rows // 2, stride=TILE), :] = from_left
    copy.wait()

    source, target = ping, pong
    for section_idx in range(sections):
        for lower, upper, row in steps(rows, part << section_idx):
            low = source[lower * TILE : (lower + 1) * TILE, :]
            if section_idx == 0:
                first = main_ref[lower * blocks : lower * blocks + 1, :]
            else:
                at = (section_idx - 1) * rows + lower
                first = firsts_ref[at : at + 1, :]
            later = jnp.where(slot == TILE - 1, first, source[lower * TILE + 1 : (lower + 1) * TILE + 1, :])
            if section_idx == 0 and counts[lower // part][0] == TILE - good:
                fourth = places[lower] + TILE - good - 1
                later = jnp.where(slot == TILE - 2, right_ref[fourth : fourth + 1, :], later)
            up = source[upper * TILE : (upper + 1) * TILE, :]
            for side in range(2):
                at = row + side
                delay = shifts_ref[section_idx, at]
                turn = (LANES - delay) & (LANES - 1)
                target[at * TILE : (at + 1) * TILE, :] = up + pltpu.roll(jnp.where(lane >= delay, low, later), turn, 1)
        source, target = target, source

    before = source[pl.ds(TILE - 1, rows, stride=TILE), :].T[LANES - WMAX :, :]
    before = jnp.where(lax.axis_index("tm") > 0, before, 0.0)
    out_ref[0:LANES, :] = boxcars(jnp.concatenate([before, tail_ref[0:LANES, :]], axis=0), band_count)
    turned[0:WMAX, :] = tail_ref[LANES : LANES + WMAX, :]
    for block in range(blocks - good):
        turned[WMAX + block * LANES : WMAX + (block + 1) * LANES, :] = source[pl.ds(block, rows, stride=TILE), :].T
    stream(turned, WMAX, (blocks - good) * LANES, out_ref, good * LANES, band_count)


def body(partial_sums, delays):
    band_count = lax.axis_size("band")
    sections = band_count.bit_length() - 1
    rows, cols = partial_sums.shape
    blocks = cols // LANES
    part = rows // band_count
    counts = right_blocks(band_count)
    params = pltpu.CompilerParams(vmem_limit_bytes=24 * 2**20)

    def struct(*shape, dtype=jnp.float32):
        return jax.ShapeDtypeStruct(shape, dtype)

    def scratch(*shape):
        return pltpu.VMEM(shape, jnp.float32)

    table = pltpu.SMEM((sections, LANES), jnp.int32)

    packed = pl.pallas_call(
        pack_kernel,
        out_shape=struct(rows * blocks, LANES),
        in_specs=[VMEM],
        out_specs=VMEM,
        compiler_params=params,
    )(partial_sums)
    mine = lax.all_to_all(packed.reshape(band_count, part * blocks, LANES), "band", split_axis=0, concat_axis=0, tiled=True)
    mine = mine.reshape(rows * blocks, LANES)

    count = lax.axis_size("tm")
    middle_at = count // 2
    wide = -(-right_rows(counts, part) // TILE) * TILE
    right, left, middle, shifts = pl.pallas_call(
        functools.partial(rims_kernel, counts, part, blocks),
        out_shape=[
            struct(wide, LANES),
            struct(rows // 2, LANES),
            struct(wide + TILE, LANES),
            struct(sections, LANES, dtype=jnp.int32),
        ],
        in_specs=[VMEM] * 2,
        out_specs=[VMEM] * 4,
        compiler_params=params,
    )(mine, delays)

    middle = lax.ppermute(middle, "tm", [(at - 1, at) for at in (middle_at, middle_at + 1)])
    right = lax.ppermute(right, "tm", [(at, at - 1) for at in range(1, count)])
    left = lax.ppermute(left, "tm", [(at - 1, at) for at in range(1, count) if at not in (middle_at, middle_at + 1)])

    merge_scratch = [scratch(rows * TILE, LANES), scratch(WMAX + cols // 2, rows), table, pltpu.SemaphoreType.DMA(())]
    tile_rows = struct(rows * TILE, LANES)
    inner, tail, firsts, outer = pl.pallas_call(
        functools.partial(inner_kernel, sections, band_count, part, blocks),
        out_shape=[
            struct(cols // 2 - LANES, rows),
            struct(LANES + WMAX, rows),
            struct((sections - 1) * rows, LANES),
            tile_rows,
        ],
        in_specs=[VMEM] * 2,
        out_specs=[VMEM] * 4,
        scratch_shapes=[scratch(rows * TILE, LANES)] + merge_scratch,
        compiler_params=params,
        cost_estimate=pl.CostEstimate(flops=2 * 10**6, bytes_accessed=4 * 2**20, transcendentals=0),
    )(shifts, mine)
    best = pl.pallas_call(
        functools.partial(outer_kernel, sections, counts, part, blocks),
        out_shape=struct(cols, rows),
        in_specs=[VMEM] * 9,
        out_specs=VMEM,
        scratch_shapes=[scratch(rows * TILE, LANES)] + merge_scratch,
        compiler_params=params,
    )(shifts, mine, right, left, middle, tail, firsts, inner, outer)

    slabs = best.reshape(band_count, cols // band_count, rows)
    slabs = lax.all_to_all(slabs, "band", split_axis=0, concat_axis=0, tiled=True)
    return slabs.transpose(1, 0, 2).reshape(cols // band_count, band_count * rows).T


def solution(mesh):
    in_specs = (P("band", "tm"), P())
    out_specs = P(None, ("tm", "band"))
    return jax.shard_map(body, mesh=mesh, in_specs=in_specs, out_specs=out_specs, check_vma=False)
```
